32 devices in a mesh: row: 2 (over x), col: 8 (over z, y), layer: 2 (over core).
Axes of the slice: x: 2, y: 2, z: 4, core: 2. Of those that a mesh axis runs over, the one named last changes fastest.
Arguments:
- flow: float32 [2048, 2048], P('row', ('col', 'layer')), as said below
- pattern: int32 [4, 4], replicated, may hold values from 0 to 1, as said below
- prune_level: int32 [4], replicated, may hold values from 1 to 8
- power: int32 [4], replicated, may hold values from 1 to 4
Outputs:
- pruned: float32 [2048, 2048], P('row', ('col', 'layer'))
The draws below stay inside these ranges and needn't reach their ends.
Inputs may be any that keep to these rules, and one draw needn't show every extreme that they name: pattern holds 0 or 1 and its diagonal is all 1; in every draw, all block rows that meet the 1024 rows of one index of row are all 1, and all block columns that meet the columns of one index of col are all 1. flow is positive.
All inputs are finite; a program needn't handle non-finite values.
Results may differ from the reference program's by a relative error of at most 0.00018.
Values sent between devices are 32-bit elements; how exact they have to be, the bound alone decides.
No kernel may reach another device: no remote copies, remote signals or barrier semaphores. Data moves between devices by JAX's collectives and lax.ppermute only.
A program may use at most 128 MiB of HBM per device.

```python
import jax
import jax.numpy as jnp
from jax import lax

BLOCK = 512
ROWS_DEV = 1024
N = 2048
NB = 4
N_ROW = 2
N_COL = 8


def draw_flow(key, part):
    first, second, third = jax.random.split(key, 3)
    base = jnp.exp(jax.random.uniform(first, (N, N), jnp.float32, jnp.log(0.5), jnp.log(2.0)))
    row_scale = jnp.exp(jax.random.uniform(second, (N, 1), jnp.float32, 0.0, jnp.log(10.0)))
    col_scale = jnp.exp(jax.random.uniform(third, (1, N), jnp.float32, 0.0, jnp.log(10.0)))
    values = base * row_scale * col_scale
    return (values / jnp.sqrt(jnp.float32(N))).astype(jnp.float32)


def draw_pattern(key, part):
    key = jax.random.fold_in(key, 7)
    first, second, third, fourth = jax.random.split(key, 4)
    hub_pick = jax.random.randint(first, (NB,), 0, 8) == 0
    rolls = jax.random.randint(second, (NB, NB), 0, 10)
    stored = jnp.where(hub_pick[None, :], rolls < 8, rolls < 2)
    places = jnp.arange(NB, dtype=jnp.int32)
    diagonal = places[:, None] == places[None, :]
    row_index = jax.random.randint(third, (), 0, N_ROW).astype(jnp.int32)
    row_low = row_index * ROWS_DEV // BLOCK
    row_high = ((row_index + 1) * ROWS_DEV - 1) // BLOCK
    dense_rows = (places >= row_low) & (places <= row_high)
    strip_width = N // N_COL
    col_index = jax.random.randint(fourth, (), 0, N_COL).astype(jnp.int32)
    col_low = col_index * strip_width // BLOCK
    col_high = ((col_index + 1) * strip_width - 1) // BLOCK
    dense_cols = (places >= col_low) & (places <= col_high)
    full = diagonal | dense_rows[:, None] | dense_cols[None, :]
    return jnp.where(full, True, stored).astype(jnp.int32)


def set_ends(drawn, stream_key, least, largest):
    dims = drawn.shape
    spot = [jax.random.randint(jax.random.fold_in(stream_key, axis), (), 0, dims[axis]) for axis in range(len(dims))]
    drawn = drawn.at[tuple(spot)].set(least)
    longest = dims.index(max(dims))
    spot[longest] = (spot[longest] + 1) % dims[longest]
    return drawn.at[tuple(spot)].set(largest)


def setup_inputs(seed: int = 0) -> dict:
    arg_keys = jax.random.split(jax.random.key(seed), 5)
    return {
        "flow": draw_flow(jax.random.fold_in(arg_keys[4], 71), 0),
        "pattern": draw_pattern(jax.random.fold_in(arg_keys[4], 71), 0),
        "prune_level": set_ends(jax.random.randint(arg_keys[2], (NB,), 1, 9), jax.random.fold_in(arg_keys[2], 1), 1, 8).astype(jnp.int32),
        "power": set_ends(jax.random.randint(arg_keys[3], (NB,), 1, 5), jax.random.fold_in(arg_keys[3], 1), 1, 4).astype(jnp.int32),
    }


def reference(flow, pattern, prune_level, power):
    stored = jnp.repeat(jnp.repeat(pattern, BLOCK, axis=0), BLOCK, axis=1)
    matrix = flow * stored.astype(jnp.float32)
    expanded = jnp.dot(matrix, matrix, precision=lax.Precision.HIGHEST, preferred_element_type=jnp.float32)
    exponents = jnp.repeat(power, BLOCK).astype(jnp.float32)
    inflated = jnp.power(expanded, exponents[None, :])
    totals = jnp.sum(inflated, axis=0)
    levels = jnp.repeat(prune_level, BLOCK).astype(jnp.float32) / 8.0
    return jnp.maximum(N * inflated / totals[None, :] - levels[None, :], 0.0)
```

```python
import jax
import jax.numpy as jnp
from jax import lax
from jax.sharding import PartitionSpec as P


def multiply(left, right):
    return jnp.dot(left, right, precision=lax.Precision.HIGH, preferred_element_type=jnp.float32)


def raise_to(value, exponent):
    square = value * value
    low = jnp.where(exponent == 1, value, square)
    high = square * jnp.where(exponent == 3, value, square)
    return jnp.where(exponent <= 2, low, high)


def general(flow, pattern, prune_level, power):
    rows, width = flow.shape
    layers = lax.axis_size("layer")
    order = rows * lax.axis_size("row")
    blocks = pattern.shape[0]
    tile_edge = order // blocks
    row_start = lax.axis_index("row") * rows
    col_start = (lax.axis_index("col") * layers + lax.axis_index("layer")) * width
    block_ids = jnp.arange(blocks, dtype=jnp.int32)
    row_ids = (row_start + jnp.arange(rows, dtype=jnp.int32)) // tile_edge
    col_ids = (col_start + jnp.arange(width, dtype=jnp.int32)) // tile_edge
    row_onehot = (row_ids[:, None] == block_ids[None, :]).astype(jnp.float32)
    col_onehot = (block_ids[:, None] == col_ids[None, :]).astype(jnp.float32)
    exact = lax.Precision.HIGHEST
    chosen = jnp.dot(
        jnp.dot(row_onehot, pattern.astype(jnp.float32), precision=exact),
        col_onehot,
        precision=exact,
    )
    masked = flow * chosen
    groups = rows // (layers * width)
    parted = masked.reshape(groups, layers, width, width)
    swapped = lax.all_to_all(parted, "layer", split_axis=1, concat_axis=3, tiled=True)
    inner_rows = swapped.reshape(groups * width, layers * width)
    strip = lax.all_gather(masked, "col", axis=1, tiled=True)
    partial_value = multiply(strip, lax.all_gather(inner_rows, "row", axis=0, tiled=True))
    expanded = lax.psum_scatter(partial_value, "layer", scatter_dimension=1, tiled=True)
    exponents = jnp.dot(power.astype(jnp.float32)[None, :], col_onehot, precision=exact)[0]
    inflated = jnp.power(expanded, exponents[None, :])
    totals = lax.psum(jnp.sum(inflated, axis=0), "row")
    levels = jnp.dot(prune_level.astype(jnp.float32)[None, :], col_onehot, precision=exact)[0] / 8.0
    return jnp.maximum(order * inflated / totals[None, :] - levels[None, :], 0.0)


def squared(flow, pattern, prune_level, power):
    rows, width = flow.shape
    half = rows // 2
    order = rows * 2
    x, c, l = lax.axis_index("row"), lax.axis_index("col"), lax.axis_index("layer")
    y, z = c % 2, c // 2

    def along_z(value, pairs):
        return lax.ppermute(value, "col", [(2 * a + b, 2 * d + b) for a, d in pairs for b in range(2)])

    def along_y(value):
        return lax.ppermute(value, "col", [(i, i ^ 1) for i in range(8)])

    def along_x(value):
        return lax.ppermute(value, "row", [(0, 1), (1, 0)])

    def across(value):
        return lax.ppermute(value, "layer", [(0, 1), (1, 0)])

    one = [(i, i ^ 1) for i in range(4)]
    two = [(i, i ^ 2) for i in range(4)]
    mid = [(1, 2), (2, 1)]
    out = [(1, 0), (2, 3)]

    own = lax.dynamic_slice_in_dim(flow, y * half, half, 0)
    rest = lax.dynamic_slice_in_dim(flow, (1 - y) * half, half, 0)
    got = along_y(rest)
    parts = []
    for piece in (own, got):
        by_two = along_z(piece, two)
        by_one = along_z(piece, one)
        by_mid = along_z(piece, mid)
        by_out = along_z(by_two, out)
        inner = (z == 1) | (z == 2)
        by_three = jnp.where(inner, by_mid, by_out)
        parts.append((piece, by_one, by_two, by_three))

    groups = flow.reshape(rows // (2 * width), 2, width, width)
    keep = lax.dynamic_index_in_dim(groups, l, 1, False).reshape(half, width)
    give = lax.dynamic_index_in_dim(groups, 1 - l, 1, False).reshape(half, width)
    near = jnp.stack([keep, across(give)])
    near_x = along_x(near)
    side = along_y(near)
    side_x = along_x(side)
    here = jnp.concatenate([near, side], axis=2)
    there = jnp.concatenate([near_x, side_x], axis=2)
    right = jnp.where(x == 0, jnp.stack([here, there], 1), jnp.stack([there, here], 1))
    right = right.reshape(2, 4, 2, width, 2 * width)
    stored = pattern[2 * x + y] * pattern[:, z]
    right = right * stored.astype(jnp.float32)[None, :, None, None, None]

    left, kept, sent = [], [], []
    for i in range(4):
        chosen = lax.dynamic_index_in_dim(right, z ^ i, 1, False)
        first = lax.dynamic_index_in_dim(chosen, y, 1, False)
        second = lax.dynamic_index_in_dim(chosen, 1 - y, 1, False)
        both = jnp.concatenate([first, second], axis=1)
        left.append(jnp.concatenate([parts[0][i], parts[1][i]], axis=1))
        kept.append(both[0])
        sent.append(both[1])
    left = jnp.concatenate(left, axis=1)
    outgoing = multiply(left, jnp.concatenate(sent, axis=0))
    product = multiply(left, jnp.concatenate(kept, axis=0)) + across(outgoing)
    inflated = raise_to(product, power[z])
    sums = jnp.sum(inflated, axis=0, keepdims=True)
    mine, other = inflated[:, :width], inflated[:, width:]
    arrived = along_y(other)
    row_sum = sums[:, :width] + along_y(sums[:, width:])
    totals = row_sum + along_x(row_sum)
    whole = jnp.where(y == 0, jnp.stack([mine, arrived]), jnp.stack([arrived, mine])).reshape(rows, width)
    level = prune_level[z].astype(jnp.float32) / 8.0
    return jnp.maximum(order * whole / totals - level, 0.0)


def solution(mesh):
    shape = dict(mesh.shape)
    special = shape == {"row": 2, "col": 8, "layer": 2}
    return jax.shard_map(
        squared if special else general,
        mesh=mesh,
        in_specs=(P("row", ("col", "layer")), P(), P(), P()),
        out_specs=P("row", ("col", "layer")),
        check_vma=False,
    )
```

```python
import jax
import jax.numpy as jnp
from jax import lax
from jax.sharding import PartitionSpec as P


def multiply(left, right):
    return jnp.dot(left, right, precision=lax.Precision.HIGH, preferred_element_type=jnp.float32)


def raise_to(value, exponent):
    square = value * value
    low = jnp.where(exponent == 1, value, square)
    high = square * jnp.where(exponent == 3, value, square)
    return jnp.where(exponent <= 2, low, high)


def general(flow, pattern, prune_level, power):
    rows, width = flow.shape
    layers = lax.axis_size("layer")
    order = rows * lax.axis_size("row")
    blocks = pattern.shape[0]
    tile_edge = order // blocks
    row_start = lax.axis_index("row") * rows
    col_start = (lax.axis_index("col") * layers + lax.axis_index("layer")) * width
    block_ids = jnp.arange(blocks, dtype=jnp.int32)
    row_ids = (row_start + jnp.arange(rows, dtype=jnp.int32)) // tile_edge
    col_ids = (col_start + jnp.arange(width, dtype=jnp.int32)) // tile_edge
    row_onehot = (row_ids[:, None] == block_ids[None, :]).astype(jnp.float32)
    col_onehot = (block_ids[:, None] == col_ids[None, :]).astype(jnp.float32)
    exact = lax.Precision.HIGHEST
    chosen = jnp.dot(
        jnp.dot(row_onehot, pattern.astype(jnp.float32), precision=exact),
        col_onehot,
        precision=exact,
    )
    masked = flow * chosen
    groups = rows // (layers * width)
    parted = masked.reshape(groups, layers, width, width)
    swapped = lax.all_to_all(parted, "layer", split_axis=1, concat_axis=3, tiled=True)
    inner_rows = swapped.reshape(groups * width, layers * width)
    strip = lax.all_gather(masked, "col", axis=1, tiled=True)
    partial_value = multiply(strip, lax.all_gather(inner_rows, "row", axis=0, tiled=True))
    expanded = lax.psum_scatter(partial_value, "layer", scatter_dimension=1, tiled=True)
    exponents = jnp.dot(power.astype(jnp.float32)[None, :], col_onehot, precision=exact)[0]
    inflated = jnp.power(expanded, exponents[None, :])
    totals = lax.psum(jnp.sum(inflated, axis=0), "row")
    levels = jnp.dot(prune_level.astype(jnp.float32)[None, :], col_onehot, precision=exact)[0] / 8.0
    return jnp.maximum(order * inflated / totals[None, :] - levels[None, :], 0.0)


def squared(flow, pattern, prune_level, power):
    rows, width = flow.shape
    half = rows // 2
    order = rows * 2
    x, c, l = lax.axis_index("row"), lax.axis_index("col"), lax.axis_index("layer")
    y, z = c % 2, c // 2

    def along_z(value, pairs, turn=0):
        return lax.ppermute(value, "col", [(2 * a + b, 2 * d + (b ^ turn)) for a, d in pairs for b in range(2)])

    def along_y(value):
        return lax.ppermute(value, "col", [(i, i ^ 1) for i in range(8)])

    def along_x(value):
        return lax.ppermute(value, "row", [(0, 1), (1, 0)])

    def across(value):
        return lax.ppermute(value, "layer", [(0, 1), (1, 0)])

    one = [(i, i ^ 1) for i in range(4)]
    two = [(i, i ^ 2) for i in range(4)]
    mid = [(1, 2), (2, 1)]
    out = [(1, 0), (2, 3)]

    def after(value, *earlier):
        return lax.optimization_barrier((value, *earlier))[0]

    def split(value):
        grouped = value.reshape(value.shape[0] // (2 * width), 2, width, width)
        return [
            lax.dynamic_index_in_dim(grouped, i, 1, False).reshape(value.shape[0] // 2, width)
            for i in (l, 1 - l)
        ]

    def both_layers(value):
        keep, give = split(value)
        return jnp.stack([keep, across(give)])

    own = lax.dynamic_slice_in_dim(flow, y * half, half, 0)
    rest = lax.dynamic_slice_in_dim(flow, (1 - y) * half, half, 0)
    two_a = along_z(own, two)
    two_b = along_z(rest, two, 1)
    beside = along_y(flow)
    far = along_x(flow)
    one_a = along_z(own, one)
    got = lax.dynamic_slice_in_dim(beside, y * half, half, 0)
    one_b = along_z(got, one)
    far_side = along_x(after(beside, far))
    near = both_layers(after(flow, beside))
    near_x = both_layers(far)
    side = both_layers(beside)
    by_two = jnp.concatenate([two_a, two_b], axis=1)
    pair = jnp.concatenate([after(own, beside), got], axis=1)
    by_out = along_z(after(by_two, one_a, near, near_x, side), out)
    by_mid = along_z(after(pair, by_two, one_a, near, near_x, side), mid)
    side_x = both_layers(far_side)
    by_one = jnp.concatenate([one_a, one_b], axis=1)

    here = jnp.concatenate([near, side], axis=2)
    there = jnp.concatenate([near_x, side_x], axis=2)
    right = jnp.where(x == 0, jnp.stack([here, there], 1), jnp.stack([there, here], 1))
    right = right.reshape(2, 4, 2, width, 2 * width)
    stored = pattern[2 * x + y] * pattern[:, z]
    right = right * stored.astype(jnp.float32)[None, :, None, None, None]
    kept, sent = [], []
    for i in range(4):
        chosen = lax.dynamic_index_in_dim(right, z ^ i, 1, False)
        first = lax.dynamic_index_in_dim(chosen, y, 1, False)
        second = lax.dynamic_index_in_dim(chosen, 1 - y, 1, False)
        both = jnp.concatenate([first, second], axis=1)
        kept.append(both[0])
        sent.append(both[1])

    left = jnp.concatenate([pair, by_one, by_two], axis=1)
    early_sent = multiply(left, jnp.concatenate(sent[:3]))
    early_kept = multiply(left, jnp.concatenate(kept[:3]))
    by_three = jnp.where((z == 1) | (z == 2), by_mid, by_out)
    by_three = after(by_three, early_sent, early_kept)
    outgoing = early_sent + multiply(by_three, sent[3])
    product = early_kept + multiply(by_three, kept[3]) + across(outgoing)
    inflated = raise_to(product, power[z])
    sums = jnp.sum(inflated, axis=0, keepdims=True)
    mine, other = inflated[:, :width], inflated[:, width:]
    arrived = along_y(other)
    row_sum = sums[:, :width] + along_y(sums[:, width:])
    totals = row_sum + along_x(row_sum)
    whole = jnp.where(y == 0, jnp.stack([mine, arrived]), jnp.stack([arrived, mine])).reshape(rows, width)
    level = prune_level[z].astype(jnp.float32) / 8.0
    return jnp.maximum(order * whole / totals - level, 0.0)


def solution(mesh):
    shape = dict(mesh.shape)
    special = shape == {"row": 2, "col": 8, "layer": 2}
    return jax.shard_map(
        squared if special else general,
        mesh=mesh,
        in_specs=(P("row", ("col", "layer")), P(), P(), P()),
        out_specs=P("row", ("col", "layer")),
        check_vma=False,
    )
```

```python
import jax
import jax.numpy as jnp
from jax import lax
from jax.sharding import PartitionSpec as P


def multiply(left, right):
    return jnp.dot(left, right, precision=lax.Precision.HIGH, preferred_element_type=jnp.float32)


def raise_to(value, exponent):
    square = value * value
    low = jnp.where(exponent == 1, value, square)
    high = square * jnp.where(exponent == 3, value, square)
    return jnp.where(exponent <= 2, low, high)


def general(flow, pattern, prune_level, power):
    rows, width = flow.shape
    layers = lax.axis_size("layer")
    order = rows * lax.axis_size("row")
    blocks = pattern.shape[0]
    tile_edge = order // blocks
    row_start = lax.axis_index("row") * rows
    col_start = (lax.axis_index("col") * layers + lax.axis_index("layer")) * width
    block_ids = jnp.arange(blocks, dtype=jnp.int32)
    row_ids = (row_start + jnp.arange(rows, dtype=jnp.int32)) // tile_edge
    col_ids = (col_start + jnp.arange(width, dtype=jnp.int32)) // tile_edge
    row_onehot = (row_ids[:, None] == block_ids[None, :]).astype(jnp.float32)
    col_onehot = (block_ids[:, None] == col_ids[None, :]).astype(jnp.float32)
    exact = lax.Precision.HIGHEST
    chosen = jnp.dot(
        jnp.dot(row_onehot, pattern.astype(jnp.float32), precision=exact),
        col_onehot,
        precision=exact,
    )
    masked = flow * chosen
    groups = rows // (layers * width)
    parted = masked.reshape(groups, layers, width, width)
    swapped = lax.all_to_all(parted, "layer", split_axis=1, concat_axis=3, tiled=True)
    inner_rows = swapped.reshape(groups * width, layers * width)
    strip = lax.all_gather(masked, "col", axis=1, tiled=True)
    partial_value = multiply(strip, lax.all_gather(inner_rows, "row", axis=0, tiled=True))
    expanded = lax.psum_scatter(partial_value, "layer", scatter_dimension=1, tiled=True)
    exponents = jnp.dot(power.astype(jnp.float32)[None, :], col_onehot, precision=exact)[0]
    inflated = jnp.power(expanded, exponents[None, :])
    totals = lax.psum(jnp.sum(inflated, axis=0), "row")
    levels = jnp.dot(prune_level.astype(jnp.float32)[None, :], col_onehot, precision=exact)[0] / 8.0
    return jnp.maximum(order * inflated / totals[None, :] - levels[None, :], 0.0)


def squared(flow, pattern, prune_level, power):
    rows, width = flow.shape
    half = rows // 2
    order = rows * 2
    x, c, l = lax.axis_index("row"), lax.axis_index("col"), lax.axis_index("layer")
    y, z = c % 2, c // 2
    p = z % 2

    def along_z(value, distance):
        return lax.ppermute(value, "col", [(i, i ^ (2 * distance)) for i in range(8)])

    def along_y(value):
        return lax.ppermute(value, "col", [(i, i ^ 1) for i in range(8)])

    def along_x(value):
        return lax.ppermute(value, "row", [(0, 1), (1, 0)])

    def across(value):
        return lax.ppermute(value, "layer", [(0, 1), (1, 0)])

    def after(value, *earlier):
        return lax.optimization_barrier((value, *earlier))[0]

    def both_layers(value):
        grouped = value.reshape(value.shape[0] // (2 * width), 2, width, width)
        keep, give = [
            lax.dynamic_index_in_dim(grouped, i, 1, False).reshape(value.shape[0] // 2, width)
            for i in (l, 1 - l)
        ]
        return jnp.stack([keep, across(give)])

    own = lax.dynamic_slice_in_dim(flow, p * half, half, 0)
    rest = lax.dynamic_slice_in_dim(flow, (1 - p) * half, half, 0)
    side_raw = along_z(flow, 1)
    two = along_z(own, 2)
    far = along_x(flow)
    own_y = along_y(own)
    three = along_z(after(rest, own_y), 3)
    two_y = along_y(two)
    far_side = along_x(after(side_raw, far))
    one = lax.dynamic_slice_in_dim(side_raw, p * half, half, 0)
    one_y = along_y(one)
    three_y = along_y(after(three, two_y, one_y))
    near = both_layers(after(flow, own_y))
    near_x = both_layers(far)
    side = both_layers(side_raw)
    side_x = both_layers(far_side)

    here = jnp.stack([near, side], axis=1)
    there = jnp.stack([near_x, side_x], axis=1)
    right = jnp.where(x == 0, jnp.stack([here, there], 2), jnp.stack([there, here], 2))
    right = right.reshape(2, 2, 4, 2, width, width)
    stored = pattern[2 * x + p][None, :] * jnp.stack([pattern[:, z], pattern[:, z ^ 1]])
    right = right * stored.astype(jnp.float32)[None, :, :, None, None, None]
    kept, sent = [], []
    for i in range(4):
        chosen = lax.dynamic_index_in_dim(right, z ^ i, 2, False)
        first = lax.dynamic_index_in_dim(chosen, y, 2, False)
        second = lax.dynamic_index_in_dim(chosen, 1 - y, 2, False)
        both = jnp.concatenate([first, second], axis=2)
        kept.append(jnp.concatenate([both[0, 0], both[0, 1]], axis=1))
        sent.append(jnp.concatenate([both[1, 0], both[1, 1]], axis=1))

    left = jnp.concatenate([own, own_y, one, one_y, two, two_y], axis=1)
    early_sent = multiply(left, jnp.concatenate(sent[:3]))
    early_kept = multiply(left, jnp.concatenate(kept[:3]))
    last = jnp.concatenate([three, after(three_y, early_sent, early_kept)], axis=1)
    outgoing = early_sent + multiply(last, sent[3])
    product = early_kept + multiply(last, kept[3]) + across(outgoing)
    mine = raise_to(product[:, :width], power[z])
    other = raise_to(product[:, width:], power[z ^ 1])
    arrived = along_z(other, 1)
    row_sum = jnp.sum(mine, axis=0, keepdims=True) + along_z(jnp.sum(other, axis=0, keepdims=True), 1)
    totals = row_sum + along_x(row_sum)
    whole = jnp.where(p == 0, jnp.stack([mine, arrived]), jnp.stack([arrived, mine])).reshape(rows, width)
    level = prune_level[z].astype(jnp.float32) / 8.0
    return jnp.maximum(order * whole / totals - level, 0.0)


def solution(mesh):
    shape = dict(mesh.shape)
    special = shape == {"row": 2, "col": 8, "layer": 2}
    return jax.shard_map(
        squared if special else general,
        mesh=mesh,
        in_specs=(P("row", ("col", "layer")), P(), P(), P()),
        out_specs=P("row", ("col", "layer")),
        check_vma=False,
    )
```

```python
import jax
import jax.numpy as jnp
from jax import lax
from jax.sharding import PartitionSpec as P


def multiply(left, right):
    return jnp.dot(left, right, precision=lax.Precision.HIGH, preferred_element_type=jnp.float32)


def raise_to(value, exponent):
    square = value * value
    low = jnp.where(exponent == 1, value, square)
    high = square * jnp.where(exponent == 3, value, square)
    return jnp.where(exponent <= 2, low, high)


def general(flow, pattern, prune_level, power):
    rows, width = flow.shape
    layers = lax.axis_size("layer")
    order = rows * lax.axis_size("row")
    blocks = pattern.shape[0]
    tile_edge = order // blocks
    row_start = lax.axis_index("row") * rows
    col_start = (lax.axis_index("col") * layers + lax.axis_index("layer")) * width
    block_ids = jnp.arange(blocks, dtype=jnp.int32)
    row_ids = (row_start + jnp.arange(rows, dtype=jnp.int32)) // tile_edge
    col_ids = (col_start + jnp.arange(width, dtype=jnp.int32)) // tile_edge
    row_onehot = (row_ids[:, None] == block_ids[None, :]).astype(jnp.float32)
    col_onehot = (block_ids[:, None] == col_ids[None, :]).astype(jnp.float32)
    exact = lax.Precision.HIGHEST
    chosen = jnp.dot(
        jnp.dot(row_onehot, pattern.astype(jnp.float32), precision=exact),
        col_onehot,
        precision=exact,
    )
    masked = flow * chosen
    groups = rows // (layers * width)
    parted = masked.reshape(groups, layers, width, width)
    swapped = lax.all_to_all(parted, "layer", split_axis=1, concat_axis=3, tiled=True)
    inner_rows = swapped.reshape(groups * width, layers * width)
    strip = lax.all_gather(masked, "col", axis=1, tiled=True)
    partial_value = multiply(strip, lax.all_gather(inner_rows, "row", axis=0, tiled=True))
    expanded = lax.psum_scatter(partial_value, "layer", scatter_dimension=1, tiled=True)
    exponents = jnp.dot(power.astype(jnp.float32)[None, :], col_onehot, precision=exact)[0]
    inflated = jnp.power(expanded, exponents[None, :])
    totals = lax.psum(jnp.sum(inflated, axis=0), "row")
    levels = jnp.dot(prune_level.astype(jnp.float32)[None, :], col_onehot, precision=exact)[0] / 8.0
    return jnp.maximum(order * inflated / totals[None, :] - levels[None, :], 0.0)


def squared(flow, pattern, prune_level, power):
    rows, width = flow.shape
    half = rows // 2
    order = rows * 2
    x, c, l = lax.axis_index("row"), lax.axis_index("col"), lax.axis_index("layer")
    y, z = c % 2, c // 2
    p = z % 2

    def along_z(value, distance):
        return lax.ppermute(value, "col", [(i, i ^ (2 * distance)) for i in range(8)])

    def along_y(value):
        return lax.ppermute(value, "col", [(i, i ^ 1) for i in range(8)])

    def along_x(value):
        return lax.ppermute(value, "row", [(0, 1), (1, 0)])

    def across(value):
        return lax.ppermute(value, "layer", [(0, 1), (1, 0)])

    def after(value, *earlier):
        return lax.optimization_barrier((value, *earlier))[0]

    def both_layers(value):
        grouped = value.reshape(value.shape[0] // (2 * width), 2, width, width)
        keep, give = [
            lax.dynamic_index_in_dim(grouped, i, 1, False).reshape(value.shape[0] // 2, width)
            for i in (l, 1 - l)
        ]
        return jnp.stack([keep, across(give)])

    def lookup(table, index):
        picked = jnp.arange(table.shape[0])[:, None] == index
        spread = jnp.broadcast_to(table.astype(jnp.float32)[:, None], (table.shape[0], width))
        return jnp.sum(jnp.where(picked, spread, 0.0), axis=0, keepdims=True)

    def in_order(mine, other):
        return jnp.where(p == 0, jnp.stack([mine, other]), jnp.stack([other, mine])).reshape(rows, width)

    own = lax.dynamic_slice_in_dim(flow, p * half, half, 0)
    rest = lax.dynamic_slice_in_dim(flow, (1 - p) * half, half, 0)
    side_raw = along_z(flow, 1)
    two = along_z(own, 2)
    far = along_x(flow)
    own_y = along_y(own)
    three = along_z(after(rest, own_y), 3)
    two_y = along_y(two)
    exponent, exponent_z, level = lookup(power, z), lookup(power, z ^ 1), lookup(prune_level, z) / 8.0
    far_side = along_x(after(side_raw, far))
    one = lax.dynamic_slice_in_dim(side_raw, p * half, half, 0)
    one_y = along_y(one)
    three_y = along_y(after(three, two_y, one_y, exponent, exponent_z, level))
    near = both_layers(after(flow, own_y))
    near_x = both_layers(far)
    side = both_layers(side_raw)
    side_x = both_layers(far_side)

    here = jnp.stack([side, near], axis=1)
    there = jnp.stack([side_x, near_x], axis=1)
    right = jnp.where(x == 0, jnp.stack([here, there], 2), jnp.stack([there, here], 2))
    right = right.reshape(2, 2, 4, 2, width, width)
    stored = pattern[2 * x + p][None, :] * jnp.stack([pattern[:, z ^ 1], pattern[:, z]])
    right = right * stored.astype(jnp.float32)[None, :, :, None, None, None]
    blocks = []
    for i in range(4):
        chosen = lax.dynamic_index_in_dim(right, z ^ i, 2, False)
        first = lax.dynamic_index_in_dim(chosen, y, 2, False)
        second = lax.dynamic_index_in_dim(chosen, 1 - y, 2, False)
        both = jnp.concatenate([first, second], axis=2)
        blocks.append([both[1, 0], both[0, 0], both[1, 1], both[0, 1]])

    own = after(own, own_y)
    left = jnp.concatenate([own, own_y, one, one_y, two, two_y], axis=1)
    wide = jnp.concatenate([jnp.concatenate(row, axis=1) for row in blocks[:3]])
    early = multiply(left, wide)
    last = jnp.concatenate([three, after(three_y, early)], axis=1)

    def finish(i):
        return early[:, i * width : (i + 1) * width] + multiply(last, blocks[3][i])

    from_core = across(finish(0))
    from_core_own = across(finish(2))
    other = raise_to(finish(1) + from_core, exponent_z)
    other_sum = jnp.sum(other, axis=0, keepdims=True)
    arrived = along_z(other, 1)
    mine = raise_to(finish(3) + from_core_own, exponent)
    sums = jnp.sum(mine, axis=0, keepdims=True)
    sums_x = along_x(sums)
    sums_xz = lax.ppermute(other_sum, ("row", "col"), [(i, i ^ 10) for i in range(16)])
    totals = sums + sums_x + sums_xz + jnp.sum(arrived, axis=0, keepdims=True)
    return jnp.maximum(order * in_order(mine, arrived) / totals - level, 0.0)


def solution(mesh):
    shape = dict(mesh.shape)
    special = shape == {"row": 2, "col": 8, "layer": 2}
    return jax.shard_map(
        squared if special else general,
        mesh=mesh,
        in_specs=(P("row", ("col", "layer")), P(), P(), P()),
        out_specs=P("row", ("col", "layer")),
        check_vma=False,
    )
```

```python
import jax
import jax.numpy as jnp
from jax import lax
from jax.sharding import PartitionSpec as P


def multiply(left, right):
    return jnp.dot(left, right, precision=lax.Precision.HIGH, preferred_element_type=jnp.float32)


def raise_to(value, exponent):
    square = value * value
    low = jnp.where(exponent == 1, value, square)
    high = square * jnp.where(exponent == 3, value, square)
    return jnp.where(exponent <= 2, low, high)


def general(flow, pattern, prune_level, power):
    rows, width = flow.shape
    layers = lax.axis_size("layer")
    order = rows * lax.axis_size("row")
    blocks = pattern.shape[0]
    tile_edge = order // blocks
    row_start = lax.axis_index("row") * rows
    col_start = (lax.axis_index("col") * layers + lax.axis_index("layer")) * width
    block_ids = jnp.arange(blocks, dtype=jnp.int32)
    row_ids = (row_start + jnp.arange(rows, dtype=jnp.int32)) // tile_edge
    col_ids = (col_start + jnp.arange(width, dtype=jnp.int32)) // tile_edge
    row_onehot = (row_ids[:, None] == block_ids[None, :]).astype(jnp.float32)
    col_onehot = (block_ids[:, None] == col_ids[None, :]).astype(jnp.float32)
    exact = lax.Precision.HIGHEST
    chosen = jnp.dot(
        jnp.dot(row_onehot, pattern.astype(jnp.float32), precision=exact),
        col_onehot,
        precision=exact,
    )
    masked = flow * chosen
    groups = rows // (layers * width)
    parted = masked.reshape(groups, layers, width, width)
    swapped = lax.all_to_all(parted, "layer", split_axis=1, concat_axis=3, tiled=True)
    inner_rows = swapped.reshape(groups * width, layers * width)
    strip = lax.all_gather(masked, "col", axis=1, tiled=True)
    partial_value = multiply(strip, lax.all_gather(inner_rows, "row", axis=0, tiled=True))
    expanded = lax.psum_scatter(partial_value, "layer", scatter_dimension=1, tiled=True)
    exponents = jnp.dot(power.astype(jnp.float32)[None, :], col_onehot, precision=exact)[0]
    inflated = jnp.power(expanded, exponents[None, :])
    totals = lax.psum(jnp.sum(inflated, axis=0), "row")
    levels = jnp.dot(prune_level.astype(jnp.float32)[None, :], col_onehot, precision=exact)[0] / 8.0
    return jnp.maximum(order * inflated / totals[None, :] - levels[None, :], 0.0)


def squared(flow, pattern, prune_level, power):
    rows, width = flow.shape
    half = rows // 2
    order = rows * 2
    x, c, l = lax.axis_index("row"), lax.axis_index("col"), lax.axis_index("layer")
    y, z = c % 2, c // 2
    p = z % 2

    def along_z(value, distance):
        return lax.ppermute(value, "col", [(i, i ^ (2 * distance)) for i in range(8)])

    def along_y(value):
        return lax.ppermute(value, "col", [(i, i ^ 1) for i in range(8)])

    def along_x(value):
        return lax.ppermute(value, "row", [(0, 1), (1, 0)])

    def across(value):
        return lax.ppermute(value, "layer", [(0, 1), (1, 0)])

    def after(value, *earlier):
        return lax.optimization_barrier((value, *earlier))[0]

    def split(value):
        grouped = value.reshape(value.shape[0] // (2 * width), 2, width, width)
        return [
            lax.dynamic_index_in_dim(grouped, i, 1, False).reshape(value.shape[0] // 2, width)
            for i in (l, 1 - l)
        ]

    def both_layers(value):
        keep, give = split(value)
        return jnp.stack([keep, across(give)])

    def lookup(table, index):
        picked = jnp.arange(table.shape[0])[:, None] == index
        spread = jnp.broadcast_to(table.astype(jnp.float32)[:, None], (table.shape[0], width))
        return jnp.sum(jnp.where(picked, spread, 0.0), axis=0, keepdims=True)

    def in_order(mine, other):
        return jnp.where(p == 0, jnp.stack([mine, other]), jnp.stack([other, mine])).reshape(rows, width)

    own = lax.dynamic_slice_in_dim(flow, p * half, half, 0)
    rest = lax.dynamic_slice_in_dim(flow, (1 - p) * half, half, 0)
    side_raw = along_z(flow, 1)
    two = along_z(own, 2)
    far = along_x(flow)
    own_y = along_y(own)
    three = along_z(after(rest, own_y), 3)
    two_y = along_y(two)
    exponent, exponent_z, level = lookup(power, z), lookup(power, z ^ 1), lookup(prune_level, z) / 8.0
    one = lax.dynamic_slice_in_dim(side_raw, p * half, half, 0)
    one_y = along_y(one)
    far_side = along_x(after(side_raw, far))
    three_y = along_y(after(three, two_y, exponent, exponent_z, level))
    near = both_layers(after(flow, own_y))
    near_x = both_layers(far)
    side = both_layers(side_raw)
    side_x = both_layers(far_side)

    here = jnp.stack([side, near], axis=1)
    there = jnp.stack([side_x, near_x], axis=1)
    right = jnp.where(x == 0, jnp.stack([here, there], 2), jnp.stack([there, here], 2))
    right = right.reshape(2, 2, 4, 2, width, width)
    stored = pattern[2 * x + p][None, :] * jnp.stack([pattern[:, z ^ 1], pattern[:, z]])
    right = right * stored.astype(jnp.float32)[None, :, :, None, None, None]
    blocks = []
    for i in range(4):
        chosen = lax.dynamic_index_in_dim(right, z ^ i, 2, False)
        first = lax.dynamic_index_in_dim(chosen, y, 2, False)
        second = lax.dynamic_index_in_dim(chosen, 1 - y, 2, False)
        both = jnp.concatenate([first, second], axis=2)
        blocks.append([both[1, 0], both[0, 0], both[1, 1], both[0, 1]])

    own = after(own, own_y)
    left = jnp.concatenate([own, own_y, one, one_y, two, two_y], axis=1)
    wide = jnp.concatenate([jnp.concatenate(row, axis=1) for row in blocks[:3]])
    early = multiply(left, wide)
    last = jnp.concatenate([three, after(three_y, early)], axis=1)

    def finish(i, block):
        return early[:, i * width : (i + 1) * width] + multiply(block, blocks[3][i])

    other = raise_to(finish(1, last) + across(finish(0, last)), exponent_z)
    other_sum = jnp.sum(other, axis=0, keepdims=True)
    arrived = along_z(other, 1)
    held = after(last, other)
    mine = raise_to(finish(3, held) + across(finish(2, held)), exponent)
    sums = jnp.sum(mine, axis=0, keepdims=True)
    sums_x = along_x(sums)
    sums_xz = lax.ppermute(other_sum, ("row", "col"), [(i, i ^ 10) for i in range(16)])
    totals = sums + sums_x + sums_xz + jnp.sum(arrived, axis=0, keepdims=True)
    return jnp.maximum(order * in_order(mine, arrived) / totals - level, 0.0)


def solution(mesh):
    shape = dict(mesh.shape)
    special = shape == {"row": 2, "col": 8, "layer": 2}
    return jax.shard_map(
        squared if special else general,
        mesh=mesh,
        in_specs=(P("row", ("col", "layer")), P(), P(), P()),
        out_specs=P("row", ("col", "layer")),
        check_vma=False,
    )
```

```python
import jax
import jax.numpy as jnp
from jax import lax
from jax.sharding import PartitionSpec as P


def multiply(left, right):
    return jnp.dot(left, right, precision=lax.Precision.HIGH, preferred_element_type=jnp.float32)


def raise_to(value, exponent):
    square = value * value
    low = jnp.where(exponent == 1, value, square)
    high = square * jnp.where(exponent == 3, value, square)
    return jnp.where(exponent <= 2, low, high)


def general(flow, pattern, prune_level, power):
    rows, width = flow.shape
    layers = lax.axis_size("layer")
    order = rows * lax.axis_size("row")
    blocks = pattern.shape[0]
    tile_edge = order // blocks
    row_start = lax.axis_index("row") * rows
    col_start = (lax.axis_index("col") * layers + lax.axis_index("layer")) * width
    block_ids = jnp.arange(blocks, dtype=jnp.int32)
    row_ids = (row_start + jnp.arange(rows, dtype=jnp.int32)) // tile_edge
    col_ids = (col_start + jnp.arange(width, dtype=jnp.int32)) // tile_edge
    row_onehot = (row_ids[:, None] == block_ids[None, :]).astype(jnp.float32)
    col_onehot = (block_ids[:, None] == col_ids[None, :]).astype(jnp.float32)
    exact = lax.Precision.HIGHEST
    chosen = jnp.dot(
        jnp.dot(row_onehot, pattern.astype(jnp.float32), precision=exact),
        col_onehot,
        precision=exact,
    )
    masked = flow * chosen
    groups = rows // (layers * width)
    parted = masked.reshape(groups, layers, width, width)
    swapped = lax.all_to_all(parted, "layer", split_axis=1, concat_axis=3, tiled=True)
    inner_rows = swapped.reshape(groups * width, layers * width)
    strip = lax.all_gather(masked, "col", axis=1, tiled=True)
    partial_value = multiply(strip, lax.all_gather(inner_rows, "row", axis=0, tiled=True))
    expanded = lax.psum_scatter(partial_value, "layer", scatter_dimension=1, tiled=True)
    exponents = jnp.dot(power.astype(jnp.float32)[None, :], col_onehot, precision=exact)[0]
    inflated = jnp.power(expanded, exponents[None, :])
    totals = lax.psum(jnp.sum(inflated, axis=0), "row")
    levels = jnp.dot(prune_level.astype(jnp.float32)[None, :], col_onehot, precision=exact)[0] / 8.0
    return jnp.maximum(order * inflated / totals[None, :] - levels[None, :], 0.0)


def squared(flow, pattern, prune_level, power):
    rows, width = flow.shape
    half = rows // 2
    order = rows * 2
    x, c, l = lax.axis_index("row"), lax.axis_index("col"), lax.axis_index("layer")
    y, z = c % 2, c // 2
    p = z % 2

    def along_z(value, distance):
        return lax.ppermute(value, "col", [(i, i ^ (2 * distance)) for i in range(8)])

    def along_y(value):
        return lax.ppermute(value, "col", [(i, i ^ 1) for i in range(8)])

    def along_x(value):
        return lax.ppermute(value, "row", [(0, 1), (1, 0)])

    def across(value):
        return lax.ppermute(value, "layer", [(0, 1), (1, 0)])

    def after(value, *earlier):
        return lax.optimization_barrier((value, *earlier))[0]

    def split(value):
        grouped = value.reshape(value.shape[0] // (2 * width), 2, width, width)
        return [
            lax.dynamic_index_in_dim(grouped, i, 1, False).reshape(value.shape[0] // 2, width)
            for i in (l, 1 - l)
        ]

    def both_layers(value):
        keep, give = split(value)
        return jnp.stack([keep, across(give)])

    def lookup(table, index):
        picked = jnp.arange(table.shape[0])[:, None] == index
        spread = jnp.broadcast_to(table.astype(jnp.float32)[:, None], (table.shape[0], width))
        return jnp.sum(jnp.where(picked, spread, 0.0), axis=0, keepdims=True)

    def in_order(mine, other):
        return jnp.where(p == 0, jnp.stack([mine, other]), jnp.stack([other, mine])).reshape(rows, width)

    own = lax.dynamic_slice_in_dim(flow, p * half, half, 0)
    rest = lax.dynamic_slice_in_dim(flow, (1 - p) * half, half, 0)
    side_raw = along_z(flow, 1)
    two = along_z(own, 2)
    far = along_x(flow)
    own_y = along_y(own)
    three = along_z(after(rest, own_y), 3)
    two_y = along_y(two)
    exponent, exponent_z, level = lookup(power, z), lookup(power, z ^ 1), lookup(prune_level, z) / 8.0
    one = lax.dynamic_slice_in_dim(side_raw, p * half, half, 0)
    one_y = along_y(one)
    far_side = along_x(after(side_raw, far, two))
    three_y = along_y(after(three, two_y, exponent, exponent_z, level))
    near = both_layers(after(flow, own_y))
    near_x = both_layers(far)
    side = both_layers(side_raw)
    side_x = both_layers(far_side)

    here = jnp.stack([side, near], axis=1)
    there = jnp.stack([side_x, near_x], axis=1)
    right = jnp.where(x == 0, jnp.stack([here, there], 2), jnp.stack([there, here], 2))
    right = right.reshape(2, 2, 4, 2, width, width)
    stored = pattern[2 * x + p][None, :] * jnp.stack([pattern[:, z ^ 1], pattern[:, z]])
    right = right * stored.astype(jnp.float32)[None, :, :, None, None, None]
    blocks = []
    for i in range(4):
        chosen = lax.dynamic_index_in_dim(right, z ^ i, 2, False)
        first = lax.dynamic_index_in_dim(chosen, y, 2, False)
        second = lax.dynamic_index_in_dim(chosen, 1 - y, 2, False)
        both = jnp.concatenate([first, second], axis=2)
        blocks.append([both[1, 0], both[0, 0], both[1, 1], both[0, 1]])

    own = after(own, own_y)
    left = jnp.concatenate([own, own_y, one, one_y, two, two_y], axis=1)
    wide = jnp.concatenate([jnp.concatenate(row, axis=1) for row in blocks[:3]])
    early = multiply(left, wide)
    last = jnp.concatenate([three, after(three_y, early)], axis=1)

    def finish(i, block):
        return early[:, i * width : (i + 1) * width] + multiply(block, blocks[3][i])

    other = raise_to(finish(1, last) + across(finish(0, last)), exponent_z)
    other_sum = jnp.sum(other, axis=0, keepdims=True)
    arrived = along_z(other, 1)
    held = after(last, other)
    mine = raise_to(finish(3, held) + across(finish(2, held)), exponent)
    sums = jnp.sum(mine, axis=0, keepdims=True)
    sums_x = along_x(sums)
    sums_xz = lax.ppermute(other_sum, ("row", "col"), [(i, i ^ 10) for i in range(16)])
    totals = sums + sums_x + sums_xz + jnp.sum(arrived, axis=0, keepdims=True)
    return jnp.maximum(order * in_order(mine, arrived) / totals - level, 0.0)


def solution(mesh):
    shape = dict(mesh.shape)
    special = shape == {"row": 2, "col": 8, "layer": 2}
    return jax.shard_map(
        squared if special else general,
        mesh=mesh,
        in_specs=(P("row", ("col", "layer")), P(), P(), P()),
        out_specs=P("row", ("col", "layer")),
        check_vma=False,
    )
```
